32 devices in a mesh: mem: 4 (over z), reg: 8 (over y, x, core).
Axes of the slice: x: 2, y: 2, z: 4, core: 2. Of those that a mesh axis runs over, the one named last changes fastest.
Arguments:
- prior_sample_set: bfloat16 [128, 69, 32, 256], P('mem', None, 'reg'), may hold values from -6 to 6
- kernel_in: bfloat16 [2, 9, 128, 69], replicated, may hold values from -0.25 to 0.25
- bias_in: float32 [2, 128], replicated, may hold values from -3 to 3
- kernel_out: bfloat16 [2, 69, 128], replicated, may hold values from -0.5 to 0.5
- observed_cell: int32 [8, 1024], replicated, may hold values from 0 to 1023
- sensor_position_variable: int32 [8, 1024], replicated, may hold values from 0 to 68
- observed_count: int32 [8], replicated, may hold values from 1 to 1024, 4096 in all
- observed_value: float32 [8, 1024], replicated, may hold values from -6 to 6
- error_variance: float32 [8, 1024], replicated, may hold values from 0.5 to 8
- radius: int32 [8], replicated, may hold values from 4 to 16
Outputs:
- analysis: bfloat16 [128, 69, 32, 256], P(None, None, 'reg', 'mem')
The draws below stay inside these ranges and needn't reach their ends.
Inputs may be any that keep to these rules, and one draw needn't show every extreme that they name: Slots 0 to observed_count - 1 of a band hold observations and the rest are unused; some band uses all 1024 slots.
All inputs are finite; a program needn't handle non-finite values.
Results may differ from the reference program's by a relative error of at most 0.0063.
Values may be sent and summed in bfloat16 or wider, within the bound.
A program may use at most 128 MiB of HBM per device.

```python
import math
import jax
import jax.numpy as jnp
import numpy as np
from jax import lax

ENSEMBLE_SIZE = 128
VARIABLE_TOTAL = 69
HID = 128
PARALLEL_LINES = 4
LON = 256
CAP = 1024
NBLK = 2
NS_ITERS = 4
NBANDS = 8
LAT = 32
PATCH_SPAN = 64
N_MEM = 4


def plant(result, rng, least, high):
    longest = result.shape.index(max(result.shape))
    spots = []
    for shift in (0, 1):
        where = [jax.random.randint(jax.random.fold_in(rng, axis), (), 0, length) for axis, length in enumerate(result.shape)]
        where[longest] = (where[longest] + shift) % result.shape[longest]
        spots.append(tuple(where))
    return result.at[spots[0]].set(least).at[spots[1]].set(high)


def block_scale(key, dims, shards, low, high):
    factor_of, own = 1.0, jax.random.fold_in(key, 6)
    for position, blocks in shards:
        draws = jnp.exp(jax.random.uniform(jax.random.fold_in(own, position), (blocks,), jnp.float32, low / len(shards), high / len(shards)))
        factor_of = factor_of * jnp.repeat(draws, dims[position] // blocks).reshape([-1 if axis == position else 1 for axis in range(len(dims))])
    return factor_of


def length_profile(amount, total, reach, slope):
    portions = [(1 << 20) // math.isqrt(rank ** slope) + 1 for rank in range(2, amount + 1)]
    rest, given = total - reach - (amount - 1), [1] * (amount - 1)
    while rest > 0:
        free = [i for i in range(amount - 1) if given[i] < reach]
        pool, remaining = sum([portions[i] for i in free]), rest
        for i in free:
            extra = min(reach - given[i], max(1, remaining * portions[i] // pool), rest)
            given[i] = given[i] + extra
            rest = rest - extra
    return np.array([reach] + given)


def ragged_sizes(rng, count, total, bound, skew):
    if count == 2:
        one = jax.random.randint(rng, (), max(1, total - bound), min(bound, total - 1) + 1)
        return jnp.stack([one, total - one])
    tallies = jnp.asarray(length_profile(count, total, bound, skew), jnp.int32)
    couples = (count - 1) // 2
    source_of, taker = tallies[1:1 + 2 * couples:2], tallies[2:2 + 2 * couples:2]
    room = jnp.minimum(source_of - 1, bound - taker)
    passed = jax.random.randint(jax.random.fold_in(rng, 1), (couples,), 0, 1 << 20) % (room + 1)
    tallies = tallies.at[1:1 + 2 * couples:2].set(source_of - passed).at[2:2 + 2 * couples:2].set(taker + passed)
    return tallies[jax.random.permutation(jax.random.fold_in(rng, 2), count)]


def gaussian(rng, dims, deviation, limit, pieces=(), kind=jnp.bfloat16):
    level = block_scale(rng, dims, pieces, -0.22, 0.18) if pieces else 1.0
    entries = jax.random.normal(rng, dims, jnp.float32) * deviation * level
    return jnp.minimum(jnp.maximum(entries, -limit), limit).astype(kind)


def setup_inputs(seed: int = 0) -> dict:
    streams_of = jax.random.split(jax.random.key(seed), 11)
    return {
        "prior_sample_set": gaussian(streams_of[0], (ENSEMBLE_SIZE, VARIABLE_TOTAL, LAT, LON), 1.0, 6.0, ((0, 4), (2, 8))),
        "kernel_in": gaussian(streams_of[1], (NBLK, 9, HID, VARIABLE_TOTAL), (9 * VARIABLE_TOTAL) ** -0.5, 0.25),
        "bias_in": gaussian(streams_of[2], (NBLK, HID), 0.5, 3.0, (), jnp.float32),
        "kernel_out": gaussian(streams_of[3], (NBLK, VARIABLE_TOTAL, HID), HID ** -0.5, 0.5),
        "observed_cell": plant(jax.random.randint(streams_of[4], (NBANDS, CAP), 0, PARALLEL_LINES * LON), jax.random.fold_in(streams_of[4], 1), 0, (PARALLEL_LINES * LON) - 1).astype(jnp.int32),
        "sensor_position_variable": plant(jax.random.randint(streams_of[5], (NBANDS, CAP), 0, VARIABLE_TOTAL), jax.random.fold_in(streams_of[5], 1), 0, VARIABLE_TOTAL - 1).astype(jnp.int32),
        "observed_count": ragged_sizes(streams_of[6], NBANDS, NBANDS * CAP // 2, CAP, 2).astype(jnp.int32),
        "observed_value": gaussian(streams_of[7], (NBANDS, CAP), 1.0, 6.0, (), jnp.float32),
        "error_variance": jnp.clip(jnp.exp(jax.random.uniform(streams_of[8], (NBANDS, CAP), jnp.float32, math.log(0.5), math.log(8.0))), 0.5, 8.0),
        "radius": plant(jax.random.randint(streams_of[9], (NBANDS,), PARALLEL_LINES, 4 * PARALLEL_LINES + 1), jax.random.fold_in(streams_of[9], 1), PARALLEL_LINES, 4 * PARALLEL_LINES).astype(jnp.int32),
    }


def apply_block(current, kernel_mix, bias_mix, kernel_back):
    padded = jnp.pad(current, ((0, 0), (1, 1), (0, 0)))
    height = current.shape[1]
    shifted_views = []
    for row_shift in range(3):
        window = padded[:, row_shift:row_shift + height, :]
        for col_shift in range(3):
            shifted_views.append(jnp.roll(window, 1 - col_shift, axis=2))
    stacked = jnp.stack(shifted_views, 0).astype(jnp.float32)
    pre_act = jnp.einsum('tfpl,thf->hpl', stacked, kernel_mix.astype(jnp.float32)) + bias_mix[:, None, None]
    hidden = jax.nn.gelu(pre_act).astype(jnp.bfloat16)
    branch = jnp.einsum('hpl,fh->fpl', hidden.astype(jnp.float32), kernel_back.astype(jnp.float32))
    return (current.astype(jnp.float32) + branch).astype(jnp.bfloat16)

def region_transform(drawn_entries, cells, counts, values, variances, radius_cells, band_first, patch_fourth, rows_dev, lon_total, quart_width, ns_iters):
    members = drawn_entries.shape[1]
    slots = drawn_entries.shape[2]
    live = jnp.arange(slots, dtype=jnp.int32)[None, :] < counts[:, None]
    band_ids = band_first + jnp.arange(3, dtype=jnp.int32)
    lat_obs = (band_ids[:, None] * rows_dev + cells // lon_total).astype(drawn_entries.dtype)
    lon_obs = (cells % lon_total).astype(drawn_entries.dtype)
    center_lat = ((band_first + 1) * rows_dev).astype(drawn_entries.dtype) + (rows_dev - 1) / 2.0
    center_lon = (patch_fourth * quart_width).astype(drawn_entries.dtype) + (quart_width - 1) / 2.0
    lat_gap = lat_obs - center_lat
    lon_gap = jnp.abs(lon_obs - center_lon)
    lon_gap = jnp.minimum(lon_gap, lon_total - lon_gap)
    spread = radius_cells.astype(drawn_entries.dtype)
    weight = jnp.where(live, jnp.exp(-(lat_gap * lat_gap + lon_gap * lon_gap) / (2.0 * spread * spread)) / variances, 0.0)
    mean_obs = lax.optimization_barrier(jnp.mean(drawn_entries, axis=1))
    perturb = drawn_entries - mean_obs[:, None, :]
    innov = values - mean_obs
    flat_pert = jnp.transpose(perturb, (1, 0, 2)).reshape(members, 3 * slots)
    flat_weight = weight.reshape(-1)
    flat_innov = innov.reshape(-1)
    identity = jnp.eye(members, dtype=drawn_entries.dtype)
    gram_matrix = jnp.dot(flat_pert * flat_weight[None, :], flat_pert.T, precision=lax.Precision.HIGHEST) + (members - 1.0) * identity
    norm_scale = jnp.sqrt(jnp.sum(gram_matrix * gram_matrix))
    scaled = gram_matrix / norm_scale

    def newton_step(step_index, carry):
        root_part, inv_part = carry
        middle = 1.5 * identity - 0.5 * jnp.dot(inv_part, root_part, precision=lax.Precision.HIGHEST)
        return (jnp.dot(root_part, middle, precision=lax.Precision.HIGHEST), jnp.dot(middle, inv_part, precision=lax.Precision.HIGHEST))
    root_part, inv_part = lax.fori_loop(0, ns_iters, newton_step, (scaled, identity))
    inverse = jnp.dot(inv_part, inv_part, precision=lax.Precision.HIGHEST) / norm_scale
    projected = jnp.dot(flat_pert, flat_weight * flat_innov, precision=lax.Precision.HIGHEST)
    mean_shift = jnp.dot(inverse, projected, precision=lax.Precision.HIGHEST)
    return jnp.sqrt(members - 1.0) * inv_part / jnp.sqrt(norm_scale) + mean_shift[:, None]

def reference(prior_sample_set, kernel_in, bias_in, kernel_out, observed_cell, sensor_position_variable, observed_count, observed_value, error_variance, radius):

    def realization_prediction(lone_realization_vector):
        current = lone_realization_vector
        for layer_index in range(NBLK):
            current = apply_block(current, kernel_in[layer_index], bias_in[layer_index], kernel_out[layer_index])
        return current
    predicted_fields = lax.map(realization_prediction, prior_sample_set)
    band_rows = jnp.arange(NBANDS, dtype=jnp.int32)[:, None]
    meridional_position = band_rows * PARALLEL_LINES + observed_cell // LON
    zonal_position = observed_cell % LON
    drawn_entries = predicted_fields[:, sensor_position_variable, meridional_position, zonal_position].astype(jnp.float32)
    drawn_entries = jnp.transpose(drawn_entries, (1, 0, 2))
    sampled_pad = jnp.pad(drawn_entries, ((1, 1), (0, 0), (0, 0)))
    cells_pad = jnp.pad(observed_cell, ((1, 1), (0, 0)))
    counts_pad = jnp.pad(observed_count, ((1, 1),))
    values_pad = jnp.pad(observed_value, ((1, 1), (0, 0)))
    variance_pad = jnp.pad(error_variance, ((1, 1), (0, 0)), constant_values=1.0)

    def region_update(region_id):
        parallel_strip = (region_id // N_MEM).astype(jnp.int32)
        patch_fourth = (region_id % N_MEM).astype(jnp.int32)
        weights_matrix = region_transform(lax.dynamic_slice_in_dim(sampled_pad, parallel_strip, 3, 0), lax.dynamic_slice_in_dim(cells_pad, parallel_strip, 3, 0), lax.dynamic_slice_in_dim(counts_pad, parallel_strip, 3, 0), lax.dynamic_slice_in_dim(values_pad, parallel_strip, 3, 0), lax.dynamic_slice_in_dim(variance_pad, parallel_strip, 3, 0), lax.dynamic_slice_in_dim(radius, parallel_strip, 1, 0)[0], parallel_strip - 1, patch_fourth, PARALLEL_LINES, LON, PATCH_SPAN, NS_ITERS)
        leading_position = jnp.zeros((), jnp.int32)
        update_patch = lax.dynamic_slice(predicted_fields, (leading_position, leading_position, (parallel_strip * PARALLEL_LINES).astype(jnp.int32), (patch_fourth * PATCH_SPAN).astype(jnp.int32)), (ENSEMBLE_SIZE, VARIABLE_TOTAL, PARALLEL_LINES, PATCH_SPAN)).astype(jnp.float32)
        mean_state = lax.optimization_barrier(jnp.mean(update_patch, axis=0))
        anomalies = update_patch - mean_state[None]
        updated = mean_state[None] + jnp.einsum('kfrq,kj->jfrq', anomalies, weights_matrix, precision=lax.Precision.HIGHEST)
        return updated.astype(jnp.bfloat16)
    regions = lax.map(region_update, jnp.arange(NBANDS * N_MEM, dtype=jnp.int32))
    regions = regions.reshape(NBANDS, N_MEM, ENSEMBLE_SIZE, VARIABLE_TOTAL, PARALLEL_LINES, PATCH_SPAN)
    regions = jnp.transpose(regions, (2, 3, 0, 4, 1, 5))
    return regions.reshape(ENSEMBLE_SIZE, VARIABLE_TOTAL, LAT, LON)
```

```python
import jax
import jax.numpy as jnp
from jax import lax
from jax.experimental import pallas as pl
from jax.experimental.pallas import tpu as pltpu
from jax.sharding import PartitionSpec as P

NBLK = 2
NS_ITERS = 4
CHUNKS = 2
FPAD = 72
STEP = 2
VMEM = 48 * 1024 * 1024


def shift_lists(axis):
    count = lax.axis_size(axis)
    forward = [(i, i + 1) for i in range(count - 1)]
    backward = [(target, source) for source, target in forward]
    return forward, backward


def conv_rows(rows, mix, bias, back):
    stacks = [
        jnp.concatenate(
            [pltpu.roll(row, 1, 1), row, pltpu.roll(row, row.shape[1] - 1, 1)], axis=0
        ).astype(jnp.bfloat16)
        for row in rows
    ]
    height = len(rows) - 2
    hid = bias.shape[0]
    sums = [bias for _ in range(height)]
    for s, stack in enumerate(stacks):
        taps = [p for p in range(3) if 0 <= s - p < height]
        part = jnp.dot(
            mix[taps[0] * hid : (taps[-1] + 1) * hid],
            stack,
            preferred_element_type=jnp.float32,
        )
        for n, p in enumerate(taps):
            sums[s - p] = sums[s - p] + part[n * hid : (n + 1) * hid]
    results = []
    for i in range(height):
        hidden = jax.nn.gelu(sums[i]).astype(jnp.bfloat16)
        results.append(rows[i + 1] + jnp.dot(back, hidden, preferred_element_type=jnp.float32))
    return results


def first_kernel(x_ref, low_ref, high_ref, mix_ref, bias_ref, back_ref, y_ref, top_ref, bot_ref, scr):
    fields, height = x_ref.shape[1], x_ref.shape[2]
    scr[...] = jnp.zeros_like(scr)
    for u in range(x_ref.shape[0]):
        x = x_ref[u].astype(jnp.float32)
        scr[u, 0, 0:fields, :] = low_ref[u].astype(jnp.float32)
        scr[u, height + 1, 0:fields, :] = high_ref[u].astype(jnp.float32)
        for p in range(height):
            scr[u, p + 1, 0:fields, :] = x[:, p, :]
    for u in range(x_ref.shape[0]):
        rows = [scr[u, s] for s in range(height + 2)]
        out = conv_rows(rows, mix_ref[...], bias_ref[...], back_ref[...])
        for p in range(height):
            y_ref[u, p] = out[p].astype(jnp.bfloat16)
        top_ref[u] = out[0].astype(jnp.bfloat16)
        bot_ref[u] = out[height - 1].astype(jnp.bfloat16)


def second_kernel(y_ref, low_ref, high_ref, mix_ref, bias_ref, back_ref, z_ref, scr):
    height = y_ref.shape[1]
    group, fields = z_ref.shape[3], z_ref.shape[1]
    step = pl.program_id(0)
    for u in range(y_ref.shape[0]):
        rows = [low_ref[u]] + [y_ref[u, p] for p in range(height)] + [high_ref[u]]
        rows = [row.astype(jnp.float32) for row in rows]
        out = conv_rows(rows, mix_ref[...], bias_ref[...], back_ref[...])
        member = step * y_ref.shape[0] + u
        for p in range(height):
            for h in range(2):
                scr[p, h, pl.ds(member, FPAD, stride=group), :] = out[p][:, h * 128 : (h + 1) * 128]

    @pl.when(step == pl.num_programs(0) - 1)
    def _():
        span = (fields // 3) * group
        keep = lax.broadcasted_iota(jnp.int32, (span, 128), 1) < 64
        for part in range(3):
            for pp in range(height // 2):
                for h in range(2):
                    a = scr[2 * pp, h, pl.ds(part * span, span), :]
                    b = scr[2 * pp + 1, h, pl.ds(part * span, span), :]
                    even = jnp.where(keep, a, pltpu.roll(b, 64, 1)).astype(jnp.bfloat16)
                    odd = jnp.where(keep, pltpu.roll(a, 64, 1), b).astype(jnp.bfloat16)
                    rows = pl.ds(part * (fields // 3), fields // 3)
                    z_ref[2 * h, rows, pp] = even.reshape(fields // 3, group, 128)
                    z_ref[2 * h + 1, rows, pp] = odd.reshape(fields // 3, group, 128)


def sample_kernel(z_ref, cell_ref, field_ref, out_ref, hot):
    quarters, fields, pairs, group, lanes = z_ref.shape
    slots = cell_ref.shape[1]
    cell = cell_ref[...]
    lane = lax.broadcasted_iota(jnp.int32, (lanes, slots), 0)
    for q in range(quarters):
        for pp in range(pairs):
            here = (2 * pp + lane // 64) * 256 + q * 64 + lane % 64
            hot[pl.ds((q * pairs + pp) * lanes, lanes), :] = jnp.where(here == cell, 1.0, 0.0).astype(
                jnp.bfloat16
            )
    wanted = field_ref[...]
    block = fields // 3

    def part(i, total):
        rows = pl.ds(i * block, block)
        left = jnp.concatenate(
            [
                z_ref[q, rows, pp].reshape(block * group, lanes)
                for q in range(quarters)
                for pp in range(pairs)
            ],
            axis=1,
        )
        for n in range(slots // 256):
            cols = slice(n * 256, (n + 1) * 256)
            found = jnp.dot(left, hot[:, cols], preferred_element_type=jnp.float32)
            piece = total[n]
            for f in range(block):
                piece = jnp.where(
                    wanted[:, cols] == i * block + f, found[f * group : (f + 1) * group], piece
                )
            total = total[:n] + (piece,) + total[n + 1 :]
        return total

    zero = tuple(jnp.zeros((group, 256), jnp.float32) for _ in range(slots // 256))
    total = lax.fori_loop(0, 3, part, zero)
    for n in range(slots // 256):
        out_ref[:, n * 256 : (n + 1) * 256] = total[n].astype(jnp.bfloat16)


def mix_kernel(*refs):
    parts, w_ref, out_ref = refs[:-2], refs[-2], refs[-1]
    fields, pairs = parts[0].shape[1], parts[0].shape[2]
    weights = w_ref[...]

    def one(f, carry):
        for pp in range(pairs):
            left = jnp.concatenate(
                [part[s, f, pp] for part in parts for s in range(part.shape[0])], axis=0
            )
            left = jnp.concatenate([left, left], axis=0)
            mixed = lax.dot_general(
                left, weights, (((0,), (0,)), ((), ())), preferred_element_type=jnp.float32
            ).astype(jnp.bfloat16)
            out_ref[f, 2 * pp] = mixed[:64]
            out_ref[f, 2 * pp + 1] = mixed[64:]
        return carry

    lax.fori_loop(0, fields, one, 0)


def call(kernel, grid, in_specs, out_shape, out_specs, scratch=(), flops=0, moved=0):
    return pl.pallas_call(
        kernel,
        grid=grid,
        in_specs=in_specs,
        out_shape=out_shape,
        out_specs=out_specs,
        scratch_shapes=list(scratch),
        compiler_params=pltpu.CompilerParams(vmem_limit_bytes=VMEM),
        cost_estimate=pl.CostEstimate(flops=flops, bytes_accessed=moved, transcendentals=0),
    )


def whole(shape):
    return pl.BlockSpec(shape, lambda i: (0,) * len(shape))


def region_transform(
    drawn_entries,
    cells,
    counts,
    values,
    variances,
    radius_cells,
    band_first,
    patch_fourth,
    rows_dev,
    lon_total,
    quart_width,
    ns_iters,
):
    members = drawn_entries.shape[1]
    slots = drawn_entries.shape[2]
    live = jnp.arange(slots, dtype=jnp.int32)[None, :] < counts[:, None]
    band_ids = band_first + jnp.arange(3, dtype=jnp.int32)
    lat_obs = (band_ids[:, None] * rows_dev + cells // lon_total).astype(drawn_entries.dtype)
    lon_obs = (cells % lon_total).astype(drawn_entries.dtype)
    center_lat = ((band_first + 1) * rows_dev).astype(drawn_entries.dtype) + (rows_dev - 1) / 2.0
    center_lon = (patch_fourth * quart_width).astype(drawn_entries.dtype) + (quart_width - 1) / 2.0
    lat_gap = lat_obs - center_lat
    lon_gap = jnp.abs(lon_obs - center_lon)
    lon_gap = jnp.minimum(lon_gap, lon_total - lon_gap)
    spread = radius_cells.astype(drawn_entries.dtype)
    weight = jnp.where(
        live,
        jnp.exp(-(lat_gap * lat_gap + lon_gap * lon_gap) / (2.0 * spread * spread)) / variances,
        0.0,
    )
    mean_obs = jnp.mean(drawn_entries, axis=1)
    perturb = drawn_entries - mean_obs[:, None, :]
    innov = values - mean_obs
    flat_pert = jnp.transpose(perturb, (1, 0, 2)).reshape(members, 3 * slots)
    flat_weight = weight.reshape(-1)
    flat_innov = innov.reshape(-1)
    identity = jnp.eye(members, dtype=drawn_entries.dtype)
    gram_matrix = (
        jnp.dot(flat_pert * flat_weight[None, :], flat_pert.T, precision=lax.Precision.HIGHEST)
        + (members - 1.0) * identity
    )
    norm_scale = jnp.sqrt(jnp.sum(gram_matrix * gram_matrix))
    scaled = gram_matrix / norm_scale

    def newton_step(step_index, carry):
        root_part, inv_part = carry
        middle = 1.5 * identity - 0.5 * jnp.dot(
            inv_part, root_part, precision=lax.Precision.HIGHEST
        )
        return (
            jnp.dot(root_part, middle, precision=lax.Precision.HIGHEST),
            jnp.dot(middle, inv_part, precision=lax.Precision.HIGHEST),
        )

    root_part, inv_part = lax.fori_loop(0, ns_iters, newton_step, (scaled, identity))
    inverse = jnp.dot(inv_part, inv_part, precision=lax.Precision.HIGHEST) / norm_scale
    projected = jnp.dot(flat_pert, flat_weight * flat_innov, precision=lax.Precision.HIGHEST)
    mean_shift = jnp.dot(inverse, projected, precision=lax.Precision.HIGHEST)
    return jnp.sqrt(members - 1.0) * inv_part / jnp.sqrt(norm_scale) + mean_shift[:, None]


def body(
    prior_sample_set,
    kernel_in,
    bias_in,
    kernel_out,
    observed_cell,
    sensor_position_variable,
    observed_count,
    observed_value,
    error_variance,
    radius,
):
    parallel_strip = lax.axis_index("reg")
    patch_fourth = lax.axis_index("mem")
    members_here, fields, rows_here, lon_total = prior_sample_set.shape
    slots = observed_cell.shape[1]
    hid = kernel_in.shape[2]
    mem_count = lax.axis_size("mem")
    members = members_here * mem_count
    group = members_here // CHUNKS
    pairs = rows_here // 2
    forward, backward = shift_lists("reg")
    room = FPAD - fields
    mixes = jnp.pad(kernel_in, ((0, 0), (0, 0), (0, 0), (0, room)))
    mixes = mixes.reshape(NBLK, 3, 3, hid, FPAD).transpose(0, 1, 3, 2, 4)
    mixes = mixes.reshape(NBLK, 3 * hid, 3 * FPAD)
    backs = jnp.pad(kernel_out, ((0, 0), (0, room), (0, 0)))
    biases = bias_in[:, :, None]
    low = lax.ppermute(prior_sample_set[:, :, rows_here - 1, :], "reg", forward)
    high = lax.ppermute(prior_sample_set[:, :, 0, :], "reg", backward)
    flops = group * rows_here * lon_total * hid * fields * 20
    bf = jnp.bfloat16
    steps = group // STEP
    weight_specs = [whole((3 * hid, 3 * FPAD)), whole((hid, 1)), whole((FPAD, hid))]
    edge = pl.BlockSpec((STEP, FPAD, lon_total), lambda i: (i, 0, 0))
    middle = pl.BlockSpec((STEP, rows_here, FPAD, lon_total), lambda i: (i, 0, 0, 0))
    firsts = []
    for c in range(CHUNKS):
        outer = pl.BlockSpec((STEP, fields, lon_total), lambda i, c=c: (i + c * steps, 0, 0))
        firsts.append(
            call(
                first_kernel,
                (steps,),
                [
                    pl.BlockSpec(
                        (STEP, fields, rows_here, lon_total), lambda i, c=c: (i + c * steps, 0, 0, 0)
                    ),
                    outer,
                    outer,
                ]
                + weight_specs,
                [
                    jax.ShapeDtypeStruct((group, rows_here, FPAD, lon_total), bf),
                    jax.ShapeDtypeStruct((group, FPAD, lon_total), bf),
                    jax.ShapeDtypeStruct((group, FPAD, lon_total), bf),
                ],
                [middle, edge, edge],
                [pltpu.VMEM((STEP, rows_here + 2, FPAD, lon_total), jnp.float32)],
                flops,
                group * 6 * fields * lon_total * 4,
            )(prior_sample_set, low, high, mixes[0], biases[0], backs[0])
        )
    edges = [
        (lax.ppermute(bot, "reg", forward), lax.ppermute(top, "reg", backward))
        for _, top, bot in firsts
    ]
    parts = []
    zshape = (mem_count, fields, pairs, group, 128)
    for c in range(CHUNKS):
        parts.append(
            call(
                second_kernel,
                (steps,),
                [middle, edge, edge] + weight_specs,
                jax.ShapeDtypeStruct(zshape, bf),
                whole(zshape),
                [pltpu.VMEM((rows_here, 2, FPAD * group, 128), jnp.float32)],
                flops,
                group * 6 * fields * lon_total * 4,
            )(firsts[c][0], edges[c][0], edges[c][1], mixes[1], biases[1], backs[1])
        )
    arrived = [lax.all_to_all(z, "mem", split_axis=0, concat_axis=0, tiled=True) for z in parts]
    field_row = lax.dynamic_slice_in_dim(sensor_position_variable, parallel_strip, 1, 0)
    cell_row = lax.dynamic_slice_in_dim(observed_cell, parallel_strip, 1, 0)
    picked = jnp.concatenate(
        [
            call(
                sample_kernel,
                (1,),
                [whole(zshape), whole((1, slots)), whole((1, slots))],
                jax.ShapeDtypeStruct((group, slots), bf),
                whole((group, slots)),
                [pltpu.VMEM((rows_here * lon_total, slots), bf)],
                2 * group * fields * 1024 * slots,
                group * fields * 2048,
            )(z, cell_row, field_row)
            for z in parts
        ],
        axis=0,
    )
    every_member = lax.all_gather(picked[None], "mem", axis=1, tiled=True)
    three_bands = jnp.concatenate(
        [
            lax.ppermute(every_member, "reg", forward),
            every_member,
            lax.ppermute(every_member, "reg", backward),
        ],
        axis=0,
    )
    cells_pad = jnp.pad(observed_cell, ((1, 1), (0, 0)))
    counts_pad = jnp.pad(observed_count, ((1, 1),))
    values_pad = jnp.pad(observed_value, ((1, 1), (0, 0)))
    variance_pad = jnp.pad(error_variance, ((1, 1), (0, 0)), constant_values=1.0)
    weights_matrix = region_transform(
        three_bands.astype(jnp.float32),
        lax.dynamic_slice_in_dim(cells_pad, parallel_strip, 3, 0),
        lax.dynamic_slice_in_dim(counts_pad, parallel_strip, 3, 0),
        lax.dynamic_slice_in_dim(values_pad, parallel_strip, 3, 0),
        lax.dynamic_slice_in_dim(variance_pad, parallel_strip, 3, 0),
        lax.dynamic_slice_in_dim(radius, parallel_strip, 1, 0)[0],
        parallel_strip - 1,
        patch_fourth,
        rows_here,
        lon_total,
        lon_total // mem_count,
        NS_ITERS,
    )
    folded = weights_matrix + (1.0 - jnp.sum(weights_matrix, axis=0, keepdims=True)) / members
    folded = folded.reshape(mem_count, CHUNKS, group, members).transpose(1, 0, 2, 3)
    folded = folded.reshape(members, members)
    coarse = folded.astype(bf)
    fine = (folded - coarse.astype(jnp.float32)).astype(bf)
    third = fields // 3
    updated = call(
        mix_kernel,
        (3,),
        [pl.BlockSpec((mem_count, third, pairs, group, 128), lambda i: (0, i, 0, 0, 0))] * CHUNKS
        + [whole((2 * members, members))],
        jax.ShapeDtypeStruct((fields, rows_here, lon_total // mem_count, members), bf),
        pl.BlockSpec((third, rows_here, lon_total // mem_count, members), lambda i: (i, 0, 0, 0)),
        (),
        4 * members * members * fields * 256,
        members * fields * 1024,
    )(*arrived, jnp.concatenate([coarse, fine], axis=0))
    return updated.transpose(3, 0, 1, 2)


def solution(mesh):
    return jax.shard_map(
        body,
        mesh=mesh,
        in_specs=(P("mem", None, "reg", None), P(), P(), P(), P(), P(), P(), P(), P(), P()),
        out_specs=P(None, None, "reg", "mem"),
        check_vma=False,
    )
```

```python
import jax
import jax.numpy as jnp
from jax import lax
from jax.experimental import pallas as pl
from jax.experimental.pallas import tpu as pltpu
from jax.sharding import PartitionSpec as P

NBLK = 2
NS_ITERS = 4
CHUNKS = 4
FPAD = 72
STEP = 2
VMEM = 48 * 1024 * 1024


def shift_lists(axis):
    count = lax.axis_size(axis)
    forward = [(i, i + 1) for i in range(count - 1)]
    backward = [(target, source) for source, target in forward]
    return forward, backward


def conv_rows(rows, mix, bias, back):
    stacks = [
        jnp.concatenate(
            [pltpu.roll(row, 1, 1), row, pltpu.roll(row, row.shape[1] - 1, 1)], axis=0
        ).astype(jnp.bfloat16)
        for row in rows
    ]
    height = len(rows) - 2
    hid = bias.shape[0]
    sums = [bias for _ in range(height)]
    for s, stack in enumerate(stacks):
        taps = [p for p in range(3) if 0 <= s - p < height]
        part = jnp.dot(
            mix[taps[0] * hid : (taps[-1] + 1) * hid],
            stack,
            preferred_element_type=jnp.float32,
        )
        for n, p in enumerate(taps):
            sums[s - p] = sums[s - p] + part[n * hid : (n + 1) * hid]
    results = []
    for i in range(height):
        hidden = jax.nn.gelu(sums[i]).astype(jnp.bfloat16)
        results.append(rows[i + 1] + jnp.dot(back, hidden, preferred_element_type=jnp.float32))
    return results


def first_kernel(x_ref, low_ref, high_ref, mix_ref, bias_ref, back_ref, _, y_ref, top_ref, bot_ref, scr):
    fields, height = x_ref.shape[1], x_ref.shape[2]
    scr[...] = jnp.zeros_like(scr)
    for u in range(x_ref.shape[0]):
        x = x_ref[u].astype(jnp.float32)
        scr[u, 0, 0:fields, :] = low_ref[u].astype(jnp.float32)
        scr[u, height + 1, 0:fields, :] = high_ref[u].astype(jnp.float32)
        for p in range(height):
            scr[u, p + 1, 0:fields, :] = x[:, p, :]
    for u in range(x_ref.shape[0]):
        rows = [scr[u, s] for s in range(height + 2)]
        out = conv_rows(rows, mix_ref[...], bias_ref[...], back_ref[...])
        for p in range(height):
            y_ref[u, p] = out[p].astype(jnp.bfloat16)
        top_ref[u] = out[0].astype(jnp.bfloat16)
        bot_ref[u] = out[height - 1].astype(jnp.bfloat16)


def second_kernel(y_ref, low_ref, high_ref, mix_ref, bias_ref, back_ref, _, z_ref, scr):
    height = y_ref.shape[1]
    group, fields = z_ref.shape[3], z_ref.shape[1]
    step = pl.program_id(0)
    for u in range(y_ref.shape[0]):
        rows = [low_ref[u]] + [y_ref[u, p] for p in range(height)] + [high_ref[u]]
        rows = [row.astype(jnp.float32) for row in rows]
        out = conv_rows(rows, mix_ref[...], bias_ref[...], back_ref[...])
        member = step * y_ref.shape[0] + u
        for p in range(height):
            for h in range(2):
                scr[p, h, pl.ds(member, FPAD, stride=group), :] = out[p][:, h * 128 : (h + 1) * 128]

    @pl.when(step == pl.num_programs(0) - 1)
    def _():
        span = (fields // 3) * group
        keep = lax.broadcasted_iota(jnp.int32, (span, 128), 1) < 64
        for part in range(3):
            for pp in range(height // 2):
                for h in range(2):
                    a = scr[2 * pp, h, pl.ds(part * span, span), :]
                    b = scr[2 * pp + 1, h, pl.ds(part * span, span), :]
                    even = jnp.where(keep, a, pltpu.roll(b, 64, 1)).astype(jnp.bfloat16)
                    odd = jnp.where(keep, pltpu.roll(a, 64, 1), b).astype(jnp.bfloat16)
                    rows = pl.ds(part * (fields // 3), fields // 3)
                    z_ref[2 * h, rows, pp] = even.reshape(fields // 3, group, 128)
                    z_ref[2 * h + 1, rows, pp] = odd.reshape(fields // 3, group, 128)


def sample_kernel(*refs):
    parts, (cell_ref, field_ref, out_ref, hot) = refs[:-4], refs[-4:]
    quarters, fields, pairs, group, lanes = parts[0].shape
    slots = cell_ref.shape[1]
    cell = cell_ref[...]
    lane = lax.broadcasted_iota(jnp.int32, (lanes, slots), 0)
    for q in range(quarters):
        for pp in range(pairs):
            here = (2 * pp + lane // 64) * 256 + q * 64 + lane % 64
            hot[pl.ds((q * pairs + pp) * lanes, lanes), :] = jnp.where(here == cell, 1.0, 0.0).astype(
                jnp.bfloat16
            )
    wanted = field_ref[...]
    block = fields // 3
    count = len(parts)

    def step(i, total):
        rows = pl.ds(i * block, block)
        left = jnp.concatenate(
            [
                jnp.concatenate(
                    [
                        part[q, rows, pp].reshape(block * group, lanes)
                        for q in range(quarters)
                        for pp in range(pairs)
                    ],
                    axis=1,
                )
                for part in parts
            ],
            axis=0,
        )
        result = []
        for n in range(slots // 256):
            cols = slice(n * 256, (n + 1) * 256)
            found = jnp.dot(left, hot[:, cols], preferred_element_type=jnp.float32)
            pieces = [total[n * count + c] for c in range(count)]
            for f in range(block):
                match = wanted[:, cols] == i * block + f
                for c in range(count):
                    start = (c * block + f) * group
                    pieces[c] = jnp.where(match, found[start : start + group], pieces[c])
            result += pieces
        return tuple(result)

    zero = tuple(jnp.zeros((group, 256), jnp.float32) for _ in range(count * (slots // 256)))
    total = lax.fori_loop(0, 3, step, zero)
    for n in range(slots // 256):
        joined = jnp.concatenate(total[n * count : (n + 1) * count], axis=0)
        out_ref[:, n * 256 : (n + 1) * 256] = joined.astype(jnp.bfloat16)


def mix_kernel(*refs):
    parts, w_ref, out_ref = refs[:-2], refs[-2], refs[-1]
    fields, pairs = parts[0].shape[1], parts[0].shape[2]
    weights = w_ref[...]

    def one(f, carry):
        for pp in range(pairs):
            left = jnp.concatenate(
                [part[s, f, pp] for part in parts for s in range(part.shape[0])], axis=0
            )
            left = jnp.concatenate([left, left], axis=0)
            mixed = lax.dot_general(
                left, weights, (((0,), (0,)), ((), ())), preferred_element_type=jnp.float32
            ).astype(jnp.bfloat16)
            out_ref[f, 2 * pp] = mixed[:64]
            out_ref[f, 2 * pp + 1] = mixed[64:]
        return carry

    lax.fori_loop(0, fields, one, 0, unroll=True)


def call(kernel, grid, in_specs, out_shape, out_specs, scratch=(), flops=0, moved=0):
    return pl.pallas_call(
        kernel,
        grid=grid,
        in_specs=in_specs,
        out_shape=out_shape,
        out_specs=out_specs,
        scratch_shapes=list(scratch),
        compiler_params=pltpu.CompilerParams(vmem_limit_bytes=VMEM),
        cost_estimate=pl.CostEstimate(flops=flops, bytes_accessed=moved, transcendentals=0),
    )


def whole(shape):
    return pl.BlockSpec(shape, lambda i: (0,) * len(shape))


def region_transform(
    drawn_entries,
    cells,
    counts,
    values,
    variances,
    radius_cells,
    band_first,
    patch_fourth,
    rows_dev,
    lon_total,
    quart_width,
    ns_iters,
):
    members = drawn_entries.shape[1]
    slots = drawn_entries.shape[2]
    live = jnp.arange(slots, dtype=jnp.int32)[None, :] < counts[:, None]
    band_ids = band_first + jnp.arange(3, dtype=jnp.int32)
    lat_obs = (band_ids[:, None] * rows_dev + cells // lon_total).astype(drawn_entries.dtype)
    lon_obs = (cells % lon_total).astype(drawn_entries.dtype)
    center_lat = ((band_first + 1) * rows_dev).astype(drawn_entries.dtype) + (rows_dev - 1) / 2.0
    center_lon = (patch_fourth * quart_width).astype(drawn_entries.dtype) + (quart_width - 1) / 2.0
    lat_gap = lat_obs - center_lat
    lon_gap = jnp.abs(lon_obs - center_lon)
    lon_gap = jnp.minimum(lon_gap, lon_total - lon_gap)
    spread = radius_cells.astype(drawn_entries.dtype)
    weight = jnp.where(
        live,
        jnp.exp(-(lat_gap * lat_gap + lon_gap * lon_gap) / (2.0 * spread * spread)) / variances,
        0.0,
    )
    mean_obs = jnp.mean(drawn_entries, axis=1)
    perturb = drawn_entries - mean_obs[:, None, :]
    innov = values - mean_obs
    flat_pert = jnp.transpose(perturb, (1, 0, 2)).reshape(members, 3 * slots)
    flat_weight = weight.reshape(-1)
    flat_innov = innov.reshape(-1)
    identity = jnp.eye(members, dtype=drawn_entries.dtype)
    gram_matrix = (
        jnp.dot(flat_pert * flat_weight[None, :], flat_pert.T, precision=lax.Precision.HIGHEST)
        + (members - 1.0) * identity
    )
    norm_scale = jnp.sqrt(jnp.sum(gram_matrix * gram_matrix))
    scaled = gram_matrix / norm_scale

    def newton_step(step_index, carry):
        root_part, inv_part = carry
        middle = 1.5 * identity - 0.5 * jnp.dot(
            inv_part, root_part, precision=lax.Precision.HIGHEST
        )
        return (
            jnp.dot(root_part, middle, precision=lax.Precision.HIGHEST),
            jnp.dot(middle, inv_part, precision=lax.Precision.HIGHEST),
        )

    root_part, inv_part = lax.fori_loop(0, ns_iters, newton_step, (scaled, identity))
    inverse = jnp.dot(inv_part, inv_part, precision=lax.Precision.HIGHEST) / norm_scale
    projected = jnp.dot(flat_pert, flat_weight * flat_innov, precision=lax.Precision.HIGHEST)
    mean_shift = jnp.dot(inverse, projected, precision=lax.Precision.HIGHEST)
    return jnp.sqrt(members - 1.0) * inv_part / jnp.sqrt(norm_scale) + mean_shift[:, None]


def body(
    prior_sample_set,
    kernel_in,
    bias_in,
    kernel_out,
    observed_cell,
    sensor_position_variable,
    observed_count,
    observed_value,
    error_variance,
    radius,
):
    parallel_strip = lax.axis_index("reg")
    patch_fourth = lax.axis_index("mem")
    members_here, fields, rows_here, lon_total = prior_sample_set.shape
    slots = observed_cell.shape[1]
    hid = kernel_in.shape[2]
    mem_count = lax.axis_size("mem")
    members = members_here * mem_count
    group = members_here // CHUNKS
    pairs = rows_here // 2
    forward, backward = shift_lists("reg")
    room = FPAD - fields
    mixes = jnp.pad(kernel_in, ((0, 0), (0, 0), (0, 0), (0, room)))
    mixes = mixes.reshape(NBLK, 3, 3, hid, FPAD).transpose(0, 1, 3, 2, 4)
    mixes = mixes.reshape(NBLK, 3 * hid, 3 * FPAD)
    backs = jnp.pad(kernel_out, ((0, 0), (0, room), (0, 0)))
    biases = bias_in[:, :, None]
    flops = group * rows_here * lon_total * hid * fields * 20
    bf = jnp.bfloat16
    steps = group // STEP
    weight_specs = [whole((3 * hid, 3 * FPAD)), whole((hid, 1)), whole((FPAD, hid))]
    weight_specs = weight_specs + [pl.BlockSpec(memory_space=pl.ANY)]
    edge = pl.BlockSpec((STEP, FPAD, lon_total), lambda i: (i, 0, 0))
    middle = pl.BlockSpec((STEP, rows_here, FPAD, lon_total), lambda i: (i, 0, 0, 0))
    outer = pl.BlockSpec((STEP, fields, lon_total), lambda i: (i, 0, 0))
    zshape = (mem_count, fields, pairs, group, 128)
    moved = group * 6 * fields * lon_total * 4

    def first(c, edge_rows, previous):
        return call(
            first_kernel,
            (steps,),
            [
                pl.BlockSpec(
                    (STEP, fields, rows_here, lon_total), lambda i: (i + c * steps, 0, 0, 0)
                ),
                outer,
                outer,
            ]
            + weight_specs,
            [
                jax.ShapeDtypeStruct((group, rows_here, FPAD, lon_total), bf),
                jax.ShapeDtypeStruct((group, FPAD, lon_total), bf),
                jax.ShapeDtypeStruct((group, FPAD, lon_total), bf),
            ],
            [middle, edge, edge],
            [pltpu.VMEM((STEP, rows_here + 2, FPAD, lon_total), jnp.float32)],
            flops,
            moved,
        )(prior_sample_set, *edge_rows, mixes[0], biases[0], backs[0], previous)

    def second(state, edge_rows, previous):
        return call(
            second_kernel,
            (steps,),
            [middle, edge, edge] + weight_specs,
            jax.ShapeDtypeStruct(zshape, bf),
            whole(zshape),
            [pltpu.VMEM((rows_here, 2, FPAD * group, 128), jnp.float32)],
            flops,
            moved,
        )(state, *edge_rows, mixes[1], biases[1], backs[1], previous)

    def exchange(bottom, top):
        return lax.ppermute(bottom, "reg", forward), lax.ppermute(top, "reg", backward)

    def spread(z):
        return lax.all_to_all(z, "mem", split_axis=0, concat_axis=0, tiled=True)

    outer_edges, ends = [], None
    for c in range(CHUNKS):
        own = prior_sample_set[c * group : (c + 1) * group]
        bottom, top = own[:, :, rows_here - 1, :], own[:, :, 0, :]
        if ends is not None:
            bottom, top, _ = lax.optimization_barrier((bottom, top, ends))
        ends = bottom
        outer_edges.append(exchange(bottom, top))
    firsts, parts, arrived = [], [], []
    previous = bias_in
    order = [(0, 0), (0, 1)] + [(1 - n % 2, n // 2 + (2 if n % 2 else 0)) for n in range(2 * CHUNKS - 4)]
    for layer, c in order + [(1, CHUNKS - 2), (1, CHUNKS - 1)]:
        if layer == 0:
            state, top, bottom = first(c, outer_edges[c], previous)
            firsts.append((state, exchange(bottom, top)))
            previous = top
        else:
            parts.append(second(*firsts[c], previous))
            previous = parts[-1]
            if c < CHUNKS - 1:
                arrived.append(spread(parts[-1]))
    field_row = lax.dynamic_slice_in_dim(sensor_position_variable, parallel_strip, 1, 0)
    cell_row = lax.dynamic_slice_in_dim(observed_cell, parallel_strip, 1, 0)
    picked = jnp.concatenate(
        [
            call(
                sample_kernel,
                (1,),
                [whole(zshape)] * 2 + [whole((1, slots)), whole((1, slots))],
                jax.ShapeDtypeStruct((2 * group, slots), bf),
                whole((2 * group, slots)),
                [pltpu.VMEM((rows_here * lon_total, slots), bf)],
                4 * group * fields * 1024 * slots,
                group * fields * 4096,
            )(parts[c], parts[c + 1], cell_row, field_row)
            for c in range(0, CHUNKS, 2)
        ],
        axis=0,
    )
    every_member = lax.all_gather(picked[None], "mem", axis=1, tiled=True)
    last, every_member = lax.optimization_barrier((parts[-1], every_member))
    arrived.append(spread(last))
    three_bands = jnp.concatenate(
        [
            lax.ppermute(every_member, "reg", forward),
            every_member,
            lax.ppermute(every_member, "reg", backward),
        ],
        axis=0,
    )
    cells_pad = jnp.pad(observed_cell, ((1, 1), (0, 0)))
    counts_pad = jnp.pad(observed_count, ((1, 1),))
    values_pad = jnp.pad(observed_value, ((1, 1), (0, 0)))
    variance_pad = jnp.pad(error_variance, ((1, 1), (0, 0)), constant_values=1.0)
    weights_matrix = region_transform(
        three_bands.astype(jnp.float32),
        lax.dynamic_slice_in_dim(cells_pad, parallel_strip, 3, 0),
        lax.dynamic_slice_in_dim(counts_pad, parallel_strip, 3, 0),
        lax.dynamic_slice_in_dim(values_pad, parallel_strip, 3, 0),
        lax.dynamic_slice_in_dim(variance_pad, parallel_strip, 3, 0),
        lax.dynamic_slice_in_dim(radius, parallel_strip, 1, 0)[0],
        parallel_strip - 1,
        patch_fourth,
        rows_here,
        lon_total,
        lon_total // mem_count,
        NS_ITERS,
    )
    folded = weights_matrix + (1.0 - jnp.sum(weights_matrix, axis=0, keepdims=True)) / members
    folded = folded.reshape(mem_count, CHUNKS, group, members).transpose(1, 0, 2, 3)
    folded = folded.reshape(members, members)
    coarse = folded.astype(bf)
    fine = (folded - coarse.astype(jnp.float32)).astype(bf)
    third = fields // 3
    updated = call(
        mix_kernel,
        (3,),
        [pl.BlockSpec((mem_count, third, pairs, group, 128), lambda i: (0, i, 0, 0, 0))] * CHUNKS
        + [whole((2 * members, members))],
        jax.ShapeDtypeStruct((fields, rows_here, lon_total // mem_count, members), bf),
        pl.BlockSpec((third, rows_here, lon_total // mem_count, members), lambda i: (i, 0, 0, 0)),
        (),
        4 * members * members * fields * 256,
        members * fields * 1024,
    )(*arrived, jnp.concatenate([coarse, fine], axis=0))
    return updated.transpose(3, 0, 1, 2)


def solution(mesh):
    return jax.shard_map(
        body,
        mesh=mesh,
        in_specs=(P("mem", None, "reg", None), P(), P(), P(), P(), P(), P(), P(), P(), P()),
        out_specs=P(None, None, "reg", "mem"),
        check_vma=False,
    )
```

```python
import jax
import jax.numpy as jnp
from jax import lax
from jax.experimental import pallas as pl
from jax.experimental.pallas import tpu as pltpu
from jax.sharding import PartitionSpec as P

NBLK = 2
NS_ITERS = 4
CHUNKS = 4
FPAD = 72
STEP = 2
VMEM = 48 * 1024 * 1024


def shift_lists(axis):
    count = lax.axis_size(axis)
    forward = [(i, i + 1) for i in range(count - 1)]
    backward = [(target, source) for source, target in forward]
    return forward, backward


def conv_rows(rows, mix, bias, back):
    stacks = [
        jnp.concatenate(
            [pltpu.roll(row, 1, 1), row, pltpu.roll(row, row.shape[1] - 1, 1)], axis=0
        ).astype(jnp.bfloat16)
        for row in rows
    ]
    height = len(rows) - 2
    hid = bias.shape[0]
    sums = [bias for _ in range(height)]
    for s, stack in enumerate(stacks):
        taps = [p for p in range(3) if 0 <= s - p < height]
        part = jnp.dot(
            mix[taps[0] * hid : (taps[-1] + 1) * hid],
            stack,
            preferred_element_type=jnp.float32,
        )
        for n, p in enumerate(taps):
            sums[s - p] = sums[s - p] + part[n * hid : (n + 1) * hid]
    results = []
    for i in range(height):
        hidden = jax.nn.gelu(sums[i]).astype(jnp.bfloat16)
        results.append(rows[i + 1] + jnp.dot(back, hidden, preferred_element_type=jnp.float32))
    return results


def forecast_kernel(
    x_ref, low_ref, high_ref, live_ref, mix_ref, bias_ref, back_ref, _, z_ref, states, scr
):
    fields, height = x_ref.shape[1], x_ref.shape[2]
    group = z_ref.shape[3]
    halo = low_ref.shape[2]
    step = pl.program_id(0)
    states[...] = jnp.zeros_like(states)
    for u in range(x_ref.shape[0]):
        row = 0
        for ref, count in ((low_ref, halo), (x_ref, height), (high_ref, halo)):
            block = ref[u].astype(jnp.float32)
            for p in range(count):
                states[u, row, 0:fields, :] = block[:, p, :]
                row += 1
    for u in range(x_ref.shape[0]):
        rows = [states[u, s] for s in range(height + 2 * halo)]
        rows = conv_rows(rows, mix_ref[0], bias_ref[0], back_ref[0])
        rows = [row.astype(jnp.bfloat16).astype(jnp.float32) for row in rows]
        rows[0] = rows[0] * live_ref[0:1, :]
        rows[-1] = rows[-1] * live_ref[1:2, :]
        out = conv_rows(rows, mix_ref[1], bias_ref[1], back_ref[1])
        member = step * x_ref.shape[0] + u
        for p in range(height):
            for h in range(2):
                scr[p, h, pl.ds(member, FPAD, stride=group), :] = out[p][:, h * 128 : (h + 1) * 128]

    @pl.when(step == pl.num_programs(0) - 1)
    def store():
        span = (fields // 3) * group
        keep = lax.broadcasted_iota(jnp.int32, (span, 128), 1) < 64
        for part in range(3):
            for pp in range(height // 2):
                for h in range(2):
                    a = scr[2 * pp, h, pl.ds(part * span, span), :]
                    b = scr[2 * pp + 1, h, pl.ds(part * span, span), :]
                    even = jnp.where(keep, a, pltpu.roll(b, 64, 1)).astype(jnp.bfloat16)
                    odd = jnp.where(keep, pltpu.roll(a, 64, 1), b).astype(jnp.bfloat16)
                    rows = pl.ds(part * (fields // 3), fields // 3)
                    z_ref[2 * h, rows, pp] = even.reshape(fields // 3, group, 128)
                    z_ref[2 * h + 1, rows, pp] = odd.reshape(fields // 3, group, 128)


def sample_kernel(*refs):
    parts, (cell_ref, field_ref, out_ref, hot) = refs[:-4], refs[-4:]
    quarters, fields, pairs, group, lanes = parts[0].shape
    slots = cell_ref.shape[1]
    cell = cell_ref[...]
    lane = lax.broadcasted_iota(jnp.int32, (lanes, slots), 0)
    for q in range(quarters):
        for pp in range(pairs):
            here = (2 * pp + lane // 64) * 256 + q * 64 + lane % 64
            hot[pl.ds((q * pairs + pp) * lanes, lanes), :] = jnp.where(here == cell, 1.0, 0.0).astype(
                jnp.bfloat16
            )
    wanted = field_ref[...]
    block = fields // 3
    count = len(parts)

    def step(i, total):
        rows = pl.ds(i * block, block)
        left = jnp.concatenate(
            [
                jnp.concatenate(
                    [
                        part[q, rows, pp].reshape(block * group, lanes)
                        for q in range(quarters)
                        for pp in range(pairs)
                    ],
                    axis=1,
                )
                for part in parts
            ],
            axis=0,
        )
        result = []
        for n in range(slots // 256):
            cols = slice(n * 256, (n + 1) * 256)
            found = jnp.dot(left, hot[:, cols], preferred_element_type=jnp.float32)
            pieces = [total[n * count + c] for c in range(count)]
            for f in range(block):
                match = wanted[:, cols] == i * block + f
                for c in range(count):
                    start = (c * block + f) * group
                    pieces[c] = jnp.where(match, found[start : start + group], pieces[c])
            result += pieces
        return tuple(result)

    zero = tuple(jnp.zeros((group, 256), jnp.float32) for _ in range(count * (slots // 256)))
    total = lax.fori_loop(0, 3, step, zero)
    for n in range(slots // 256):
        joined = jnp.concatenate(total[n * count : (n + 1) * count], axis=0)
        out_ref[:, n * 256 : (n + 1) * 256] = joined.astype(jnp.bfloat16)


def mix_kernel(*refs):
    parts, w_ref, out_ref = refs[:-2], refs[-2], refs[-1]
    fields, pairs = parts[0].shape[1], parts[0].shape[2]
    weights = w_ref[...]

    def one(f, carry):
        for pp in range(pairs):
            left = jnp.concatenate(
                [part[s, f, pp] for part in parts for s in range(part.shape[0])], axis=0
            )
            left = jnp.concatenate([left, left], axis=0)
            mixed = lax.dot_general(
                left, weights, (((0,), (0,)), ((), ())), preferred_element_type=jnp.float32
            ).astype(jnp.bfloat16)
            out_ref[f, 2 * pp] = mixed[:64]
            out_ref[f, 2 * pp + 1] = mixed[64:]
        return carry

    lax.fori_loop(0, fields, one, 0, unroll=True)


def call(kernel, grid, in_specs, out_shape, out_specs, scratch=(), flops=0, moved=0):
    return pl.pallas_call(
        kernel,
        grid=grid,
        in_specs=in_specs,
        out_shape=out_shape,
        out_specs=out_specs,
        scratch_shapes=list(scratch),
        compiler_params=pltpu.CompilerParams(vmem_limit_bytes=VMEM),
        cost_estimate=pl.CostEstimate(flops=flops, bytes_accessed=moved, transcendentals=0),
    )


def whole(shape):
    return pl.BlockSpec(shape, lambda i: (0,) * len(shape))


def region_transform(
    drawn_entries,
    cells,
    counts,
    values,
    variances,
    radius_cells,
    band_first,
    patch_fourth,
    rows_dev,
    lon_total,
    quart_width,
    ns_iters,
):
    members = drawn_entries.shape[1]
    slots = drawn_entries.shape[2]
    live = jnp.arange(slots, dtype=jnp.int32)[None, :] < counts[:, None]
    band_ids = band_first + jnp.arange(3, dtype=jnp.int32)
    lat_obs = (band_ids[:, None] * rows_dev + cells // lon_total).astype(drawn_entries.dtype)
    lon_obs = (cells % lon_total).astype(drawn_entries.dtype)
    center_lat = ((band_first + 1) * rows_dev).astype(drawn_entries.dtype) + (rows_dev - 1) / 2.0
    center_lon = (patch_fourth * quart_width).astype(drawn_entries.dtype) + (quart_width - 1) / 2.0
    lat_gap = lat_obs - center_lat
    lon_gap = jnp.abs(lon_obs - center_lon)
    lon_gap = jnp.minimum(lon_gap, lon_total - lon_gap)
    spread = radius_cells.astype(drawn_entries.dtype)
    weight = jnp.where(
        live,
        jnp.exp(-(lat_gap * lat_gap + lon_gap * lon_gap) / (2.0 * spread * spread)) / variances,
        0.0,
    )
    mean_obs = jnp.mean(drawn_entries, axis=1)
    perturb = drawn_entries - mean_obs[:, None, :]
    innov = values - mean_obs
    flat_pert = jnp.transpose(perturb, (1, 0, 2)).reshape(members, 3 * slots)
    flat_weight = weight.reshape(-1)
    flat_innov = innov.reshape(-1)
    identity = jnp.eye(members, dtype=drawn_entries.dtype)
    gram_matrix = (
        jnp.dot(flat_pert * flat_weight[None, :], flat_pert.T, precision=lax.Precision.HIGHEST)
        + (members - 1.0) * identity
    )
    norm_scale = jnp.sqrt(jnp.sum(gram_matrix * gram_matrix))
    scaled = gram_matrix / norm_scale

    def newton_step(step_index, carry):
        root_part, inv_part = carry
        middle = 1.5 * identity - 0.5 * jnp.dot(
            inv_part, root_part, precision=lax.Precision.HIGHEST
        )
        return (
            jnp.dot(root_part, middle, precision=lax.Precision.HIGHEST),
            jnp.dot(middle, inv_part, precision=lax.Precision.HIGHEST),
        )

    root_part, inv_part = lax.fori_loop(0, ns_iters, newton_step, (scaled, identity))
    inverse = jnp.dot(inv_part, inv_part, precision=lax.Precision.HIGHEST) / norm_scale
    projected = jnp.dot(flat_pert, flat_weight * flat_innov, precision=lax.Precision.HIGHEST)
    mean_shift = jnp.dot(inverse, projected, precision=lax.Precision.HIGHEST)
    return jnp.sqrt(members - 1.0) * inv_part / jnp.sqrt(norm_scale) + mean_shift[:, None]


def body(
    prior_sample_set,
    kernel_in,
    bias_in,
    kernel_out,
    observed_cell,
    sensor_position_variable,
    observed_count,
    observed_value,
    error_variance,
    radius,
):
    parallel_strip = lax.axis_index("reg")
    patch_fourth = lax.axis_index("mem")
    members_here, fields, rows_here, lon_total = prior_sample_set.shape
    slots = observed_cell.shape[1]
    hid = kernel_in.shape[2]
    mem_count = lax.axis_size("mem")
    members = members_here * mem_count
    group = members_here // CHUNKS
    pairs = rows_here // 2
    forward, backward = shift_lists("reg")
    room = FPAD - fields
    mixes = jnp.pad(kernel_in, ((0, 0), (0, 0), (0, 0), (0, room)))
    mixes = mixes.reshape(NBLK, 3, 3, hid, FPAD).transpose(0, 1, 3, 2, 4)
    mixes = mixes.reshape(NBLK, 3 * hid, 3 * FPAD)
    backs = jnp.pad(kernel_out, ((0, 0), (0, room), (0, 0)))
    biases = bias_in[:, :, None]
    flops = group * rows_here * lon_total * hid * fields * 20
    bf = jnp.bfloat16
    steps = group // STEP
    halo = 2
    live = jnp.stack([parallel_strip > 0, parallel_strip < lax.axis_size("reg") - 1])
    live = jnp.broadcast_to(live.astype(jnp.float32)[:, None], (2, lon_total))
    outer = pl.BlockSpec((STEP, fields, halo, lon_total), lambda i: (i, 0, 0, 0))
    zshape = (mem_count, fields, pairs, group, 128)

    def forecast(c, low, high, previous):
        return call(
            forecast_kernel,
            (steps,),
            [
                pl.BlockSpec(
                    (STEP, fields, rows_here, lon_total), lambda i: (i + c * steps, 0, 0, 0)
                ),
                outer,
                outer,
                whole(live.shape),
                whole(mixes.shape),
                whole(biases.shape),
                whole(backs.shape),
                pl.BlockSpec(memory_space=pl.ANY),
            ],
            jax.ShapeDtypeStruct(zshape, bf),
            whole(zshape),
            [
                pltpu.VMEM((STEP, rows_here + 2 * halo, FPAD, lon_total), jnp.float32),
                pltpu.VMEM((rows_here, 2, FPAD * group, 128), jnp.float32),
            ],
            flops * 5 // 2,
            group * 12 * fields * lon_total * 2,
        )(prior_sample_set, low, high, live, mixes, biases, backs, previous)

    def spread(z):
        return lax.all_to_all(z, "mem", split_axis=0, concat_axis=0, tiled=True)

    edges = []
    for c in range(CHUNKS):
        own = prior_sample_set[c * group : (c + 1) * group]
        low = lax.ppermute(own[:, :, rows_here - halo :, :], "reg", forward)
        high = lax.ppermute(own[:, :, :halo, :], "reg", backward)
        edges.append((low, high))
    parts, arrived = [], []
    previous = bias_in
    for c in range(CHUNKS):
        parts.append(forecast(c, *edges[c], previous))
        previous = parts[-1]
        if c < CHUNKS - 1:
            arrived.append(spread(parts[-1]))
    field_row = lax.dynamic_slice_in_dim(sensor_position_variable, parallel_strip, 1, 0)
    cell_row = lax.dynamic_slice_in_dim(observed_cell, parallel_strip, 1, 0)
    picked = jnp.concatenate(
        [
            call(
                sample_kernel,
                (1,),
                [whole(zshape)] * 2 + [whole((1, slots)), whole((1, slots))],
                jax.ShapeDtypeStruct((2 * group, slots), bf),
                whole((2 * group, slots)),
                [pltpu.VMEM((rows_here * lon_total, slots), bf)],
                4 * group * fields * 1024 * slots,
                group * fields * 4096,
            )(parts[c], parts[c + 1], cell_row, field_row)
            for c in range(0, CHUNKS, 2)
        ],
        axis=0,
    )
    every_member = lax.all_gather(picked[None], "mem", axis=1, tiled=True)
    last, every_member = lax.optimization_barrier((parts[-1], every_member))
    arrived.append(spread(last))
    three_bands = jnp.concatenate(
        [
            lax.ppermute(every_member, "reg", forward),
            every_member,
            lax.ppermute(every_member, "reg", backward),
        ],
        axis=0,
    )
    cells_pad = jnp.pad(observed_cell, ((1, 1), (0, 0)))
    counts_pad = jnp.pad(observed_count, ((1, 1),))
    values_pad = jnp.pad(observed_value, ((1, 1), (0, 0)))
    variance_pad = jnp.pad(error_variance, ((1, 1), (0, 0)), constant_values=1.0)
    weights_matrix = region_transform(
        three_bands.astype(jnp.float32),
        lax.dynamic_slice_in_dim(cells_pad, parallel_strip, 3, 0),
        lax.dynamic_slice_in_dim(counts_pad, parallel_strip, 3, 0),
        lax.dynamic_slice_in_dim(values_pad, parallel_strip, 3, 0),
        lax.dynamic_slice_in_dim(variance_pad, parallel_strip, 3, 0),
        lax.dynamic_slice_in_dim(radius, parallel_strip, 1, 0)[0],
        parallel_strip - 1,
        patch_fourth,
        rows_here,
        lon_total,
        lon_total // mem_count,
        NS_ITERS,
    )
    folded = weights_matrix + (1.0 - jnp.sum(weights_matrix, axis=0, keepdims=True)) / members
    folded = folded.reshape(mem_count, CHUNKS, group, members).transpose(1, 0, 2, 3)
    folded = folded.reshape(members, members)
    coarse = folded.astype(bf)
    fine = (folded - coarse.astype(jnp.float32)).astype(bf)
    third = fields // 3
    updated = call(
        mix_kernel,
        (3,),
        [pl.BlockSpec((mem_count, third, pairs, group, 128), lambda i: (0, i, 0, 0, 0))] * CHUNKS
        + [whole((2 * members, members))],
        jax.ShapeDtypeStruct((fields, rows_here, lon_total // mem_count, members), bf),
        pl.BlockSpec((third, rows_here, lon_total // mem_count, members), lambda i: (i, 0, 0, 0)),
        (),
        4 * members * members * fields * 256,
        members * fields * 1024,
    )(*arrived, jnp.concatenate([coarse, fine], axis=0))
    return updated.transpose(3, 0, 1, 2)


def solution(mesh):
    return jax.shard_map(
        body,
        mesh=mesh,
        in_specs=(P("mem", None, "reg", None), P(), P(), P(), P(), P(), P(), P(), P(), P()),
        out_specs=P(None, None, "reg", "mem"),
        check_vma=False,
    )
```

```python
import jax
import jax.numpy as jnp
from jax import lax
from jax.experimental import pallas as pl
from jax.experimental.pallas import tpu as pltpu
from jax.sharding import PartitionSpec as P

NBLK = 2
NS_ITERS = 4
CHUNKS = 4
FPAD = 72
STEP = 2
VMEM = 48 * 1024 * 1024


def shift_lists(axis):
    count = lax.axis_size(axis)
    forward = [(i, i + 1) for i in range(count - 1)]
    backward = [(target, source) for source, target in forward]
    return forward, backward


def conv_rows(rows, mix, bias, back):
    stacks = [
        jnp.concatenate(
            [pltpu.roll(row, 1, 1), row, pltpu.roll(row, row.shape[1] - 1, 1)], axis=0
        ).astype(jnp.bfloat16)
        for row in rows
    ]
    height = len(rows) - 2
    hid = bias.shape[0]
    sums = [bias for _ in range(height)]
    for s, stack in enumerate(stacks):
        taps = [p for p in range(3) if 0 <= s - p < height]
        part = jnp.dot(
            mix[taps[0] * hid : (taps[-1] + 1) * hid],
            stack,
            preferred_element_type=jnp.float32,
        )
        for n, p in enumerate(taps):
            sums[s - p] = sums[s - p] + part[n * hid : (n + 1) * hid]
    results = []
    for i in range(height):
        hidden = jax.nn.gelu(sums[i]).astype(jnp.bfloat16)
        results.append(rows[i + 1] + jnp.dot(back, hidden, preferred_element_type=jnp.float32))
    return results


def forecast_kernel(
    x_ref, low_ref, high_ref, live_ref, mix_ref, bias_ref, back_ref, _, z_ref, states, scr
):
    fields, height = x_ref.shape[1], x_ref.shape[2]
    group = z_ref.shape[3]
    halo = low_ref.shape[2]
    step = pl.program_id(0)
    states[...] = jnp.zeros_like(states)
    for u in range(x_ref.shape[0]):
        row = 0
        for ref, count in ((low_ref, halo), (x_ref, height), (high_ref, halo)):
            block = ref[u].astype(jnp.float32)
            for p in range(count):
                states[u, row, 0:fields, :] = block[:, p, :]
                row += 1
    for u in range(x_ref.shape[0]):
        rows = [states[u, s] for s in range(height + 2 * halo)]
        rows = conv_rows(rows, mix_ref[0], bias_ref[0], back_ref[0])
        rows = [row.astype(jnp.bfloat16).astype(jnp.float32) for row in rows]
        rows[0] = rows[0] * live_ref[0:1, :]
        rows[-1] = rows[-1] * live_ref[1:2, :]
        out = conv_rows(rows, mix_ref[1], bias_ref[1], back_ref[1])
        member = step * x_ref.shape[0] + u
        for p in range(height):
            for h in range(2):
                scr[p, h, pl.ds(member, FPAD, stride=group), :] = out[p][:, h * 128 : (h + 1) * 128]

    @pl.when(step == pl.num_programs(0) - 1)
    def store():
        span = (fields // 3) * group
        keep = lax.broadcasted_iota(jnp.int32, (span, 128), 1) < 64
        for part in range(3):
            for pp in range(height // 2):
                for h in range(2):
                    a = scr[2 * pp, h, pl.ds(part * span, span), :]
                    b = scr[2 * pp + 1, h, pl.ds(part * span, span), :]
                    even = jnp.where(keep, a, pltpu.roll(b, 64, 1)).astype(jnp.bfloat16)
                    odd = jnp.where(keep, pltpu.roll(a, 64, 1), b).astype(jnp.bfloat16)
                    rows = pl.ds(part * (fields // 3), fields // 3)
                    z_ref[2 * h, rows, pp] = even.reshape(fields // 3, group, 128)
                    z_ref[2 * h + 1, rows, pp] = odd.reshape(fields // 3, group, 128)


def sample_kernel(*refs):
    parts, (cell_ref, field_ref, out_ref, hot) = refs[:-4], refs[-4:]
    quarters, fields, pairs, group, lanes = parts[0].shape
    slots = cell_ref.shape[1]
    cell = cell_ref[...]
    lane = lax.broadcasted_iota(jnp.int32, (lanes, slots), 0)
    for q in range(quarters):
        for pp in range(pairs):
            here = (2 * pp + lane // 64) * 256 + q * 64 + lane % 64
            hot[pl.ds((q * pairs + pp) * lanes, lanes), :] = jnp.where(here == cell, 1.0, 0.0).astype(
                jnp.bfloat16
            )
    wanted = field_ref[...]
    block = fields // 3
    count = len(parts)

    def step(i, total):
        rows = pl.ds(i * block, block)
        left = jnp.concatenate(
            [
                jnp.concatenate(
                    [
                        part[q, rows, pp].reshape(block * group, lanes)
                        for q in range(quarters)
                        for pp in range(pairs)
                    ],
                    axis=1,
                )
                for part in parts
            ],
            axis=0,
        )
        result = []
        for n in range(slots // 256):
            cols = slice(n * 256, (n + 1) * 256)
            found = jnp.dot(left, hot[:, cols], preferred_element_type=jnp.float32)
            pieces = [total[n * count + c] for c in range(count)]
            for f in range(block):
                match = wanted[:, cols] == i * block + f
                for c in range(count):
                    start = (c * block + f) * group
                    pieces[c] = jnp.where(match, found[start : start + group], pieces[c])
            result += pieces
        return tuple(result)

    zero = tuple(jnp.zeros((group, 256), jnp.float32) for _ in range(count * (slots // 256)))
    total = lax.fori_loop(0, 3, step, zero)
    for n in range(slots // 256):
        joined = jnp.concatenate(total[n * count : (n + 1) * count], axis=0)
        out_ref[:, n * 256 : (n + 1) * 256] = joined.astype(jnp.bfloat16)


def mix_kernel(*refs):
    parts, w_ref, out_ref = refs[:-2], refs[-2], refs[-1]
    fields, pairs = parts[0].shape[1], parts[0].shape[2]
    weights = w_ref[...]

    def one(f, carry):
        for pp in range(pairs):
            left = jnp.concatenate(
                [part[s, f, pp] for part in parts for s in range(part.shape[0])], axis=0
            )
            left = jnp.concatenate([left, left], axis=0)
            mixed = lax.dot_general(
                left, weights, (((0,), (0,)), ((), ())), preferred_element_type=jnp.float32
            ).astype(jnp.bfloat16)
            out_ref[f, 2 * pp] = mixed[:64]
            out_ref[f, 2 * pp + 1] = mixed[64:]
        return carry

    lax.fori_loop(0, fields, one, 0, unroll=True)


def call(kernel, grid, in_specs, out_shape, out_specs, scratch=(), flops=0, moved=0):
    return pl.pallas_call(
        kernel,
        grid=grid,
        in_specs=in_specs,
        out_shape=out_shape,
        out_specs=out_specs,
        scratch_shapes=list(scratch),
        compiler_params=pltpu.CompilerParams(vmem_limit_bytes=VMEM),
        cost_estimate=pl.CostEstimate(flops=flops, bytes_accessed=moved, transcendentals=0),
    )


def whole(shape):
    return pl.BlockSpec(shape, lambda i: (0,) * len(shape))


def region_transform(
    drawn_entries,
    cells,
    counts,
    values,
    variances,
    radius_cells,
    band_first,
    patch_fourth,
    rows_dev,
    lon_total,
    quart_width,
    ns_iters,
):
    members = drawn_entries.shape[1]
    slots = drawn_entries.shape[2]
    live = jnp.arange(slots, dtype=jnp.int32)[None, :] < counts[:, None]
    band_ids = band_first + jnp.arange(3, dtype=jnp.int32)
    lat_obs = (band_ids[:, None] * rows_dev + cells // lon_total).astype(drawn_entries.dtype)
    lon_obs = (cells % lon_total).astype(drawn_entries.dtype)
    center_lat = ((band_first + 1) * rows_dev).astype(drawn_entries.dtype) + (rows_dev - 1) / 2.0
    center_lon = (patch_fourth * quart_width).astype(drawn_entries.dtype) + (quart_width - 1) / 2.0
    lat_gap = lat_obs - center_lat
    lon_gap = jnp.abs(lon_obs - center_lon)
    lon_gap = jnp.minimum(lon_gap, lon_total - lon_gap)
    spread = radius_cells.astype(drawn_entries.dtype)
    weight = jnp.where(
        live,
        jnp.exp(-(lat_gap * lat_gap + lon_gap * lon_gap) / (2.0 * spread * spread)) / variances,
        0.0,
    )
    mean_obs = jnp.mean(drawn_entries, axis=1)
    perturb = drawn_entries - mean_obs[:, None, :]
    innov = values - mean_obs
    flat_pert = jnp.transpose(perturb, (1, 0, 2)).reshape(members, 3 * slots)
    flat_weight = weight.reshape(-1)
    flat_innov = innov.reshape(-1)
    identity = jnp.eye(members, dtype=drawn_entries.dtype)
    gram_matrix = (
        jnp.dot(flat_pert * flat_weight[None, :], flat_pert.T, precision=lax.Precision.HIGHEST)
        + (members - 1.0) * identity
    )
    norm_scale = jnp.sqrt(jnp.sum(gram_matrix * gram_matrix))
    scaled = gram_matrix / norm_scale

    def newton_step(step_index, carry):
        root_part, inv_part = carry
        middle = 1.5 * identity - 0.5 * jnp.dot(
            inv_part, root_part, precision=lax.Precision.HIGHEST
        )
        return (
            jnp.dot(root_part, middle, precision=lax.Precision.HIGHEST),
            jnp.dot(middle, inv_part, precision=lax.Precision.HIGHEST),
        )

    root_part, inv_part = lax.fori_loop(0, ns_iters, newton_step, (scaled, identity))
    inverse = jnp.dot(inv_part, inv_part, precision=lax.Precision.HIGHEST) / norm_scale
    projected = jnp.dot(flat_pert, flat_weight * flat_innov, precision=lax.Precision.HIGHEST)
    mean_shift = jnp.dot(inverse, projected, precision=lax.Precision.HIGHEST)
    return jnp.sqrt(members - 1.0) * inv_part / jnp.sqrt(norm_scale) + mean_shift[:, None]


def body(
    prior_sample_set,
    kernel_in,
    bias_in,
    kernel_out,
    observed_cell,
    sensor_position_variable,
    observed_count,
    observed_value,
    error_variance,
    radius,
):
    parallel_strip = lax.axis_index("reg")
    patch_fourth = lax.axis_index("mem")
    members_here, fields, rows_here, lon_total = prior_sample_set.shape
    slots = observed_cell.shape[1]
    hid = kernel_in.shape[2]
    mem_count = lax.axis_size("mem")
    members = members_here * mem_count
    group = members_here // CHUNKS
    pairs = rows_here // 2
    forward, backward = shift_lists("reg")
    room = FPAD - fields
    mixes = jnp.pad(kernel_in, ((0, 0), (0, 0), (0, 0), (0, room)))
    mixes = mixes.reshape(NBLK, 3, 3, hid, FPAD).transpose(0, 1, 3, 2, 4)
    mixes = mixes.reshape(NBLK, 3 * hid, 3 * FPAD)
    backs = jnp.pad(kernel_out, ((0, 0), (0, room), (0, 0)))
    biases = bias_in[:, :, None]
    flops = group * rows_here * lon_total * hid * fields * 20
    bf = jnp.bfloat16
    steps = group // STEP
    halo = 2
    live = jnp.stack([parallel_strip > 0, parallel_strip < lax.axis_size("reg") - 1])
    live = jnp.broadcast_to(live.astype(jnp.float32)[:, None], (2, lon_total))
    outer = pl.BlockSpec((STEP, fields, halo, lon_total), lambda i: (i, 0, 0, 0))
    zshape = (mem_count, fields, pairs, group, 128)

    def forecast(c, low, high, previous):
        return call(
            forecast_kernel,
            (steps,),
            [
                pl.BlockSpec(
                    (STEP, fields, rows_here, lon_total), lambda i: (i + c * steps, 0, 0, 0)
                ),
                outer,
                outer,
                whole(live.shape),
                whole(mixes.shape),
                whole(biases.shape),
                whole(backs.shape),
                pl.BlockSpec(memory_space=pl.ANY),
            ],
            jax.ShapeDtypeStruct(zshape, bf),
            whole(zshape),
            [
                pltpu.VMEM((STEP, rows_here + 2 * halo, FPAD, lon_total), jnp.float32),
                pltpu.VMEM((rows_here, 2, FPAD * group, 128), jnp.float32),
            ],
            flops * 5 // 2,
            group * 12 * fields * lon_total * 2,
        )(prior_sample_set, low, high, live, mixes, biases, backs, previous)

    def spread(z):
        return lax.all_to_all(z, "mem", split_axis=0, concat_axis=0, tiled=True)

    edges = []
    for c in range(CHUNKS):
        own = prior_sample_set[c * group : (c + 1) * group]
        low = lax.ppermute(own[:, :, rows_here - halo :, :], "reg", forward)
        high = lax.ppermute(own[:, :, :halo, :], "reg", backward)
        edges.append((low, high))
    parts, arrived = [], []
    previous = bias_in
    for c in range(CHUNKS):
        parts.append(forecast(c, *edges[c], previous))
        if c < CHUNKS - 1:
            arrived.append(spread(parts[-1]))
        previous = arrived[c - 1] if c > 0 else parts[0]
    field_row = lax.dynamic_slice_in_dim(sensor_position_variable, parallel_strip, 1, 0)
    cell_row = lax.dynamic_slice_in_dim(observed_cell, parallel_strip, 1, 0)
    picked = jnp.concatenate(
        [
            call(
                sample_kernel,
                (1,),
                [whole(zshape)] * 2 + [whole((1, slots)), whole((1, slots))],
                jax.ShapeDtypeStruct((2 * group, slots), bf),
                whole((2 * group, slots)),
                [pltpu.VMEM((rows_here * lon_total, slots), bf)],
                4 * group * fields * 1024 * slots,
                group * fields * 4096,
            )(parts[c], parts[c + 1], cell_row, field_row)
            for c in range(0, CHUNKS, 2)
        ],
        axis=0,
    )
    every_member = lax.all_gather(picked[None], "mem", axis=1, tiled=True)
    last, every_member = lax.optimization_barrier((parts[-1], every_member))
    arrived.append(spread(last))
    three_bands = jnp.concatenate(
        [
            lax.ppermute(every_member, "reg", forward),
            every_member,
            lax.ppermute(every_member, "reg", backward),
        ],
        axis=0,
    )
    cells_pad = jnp.pad(observed_cell, ((1, 1), (0, 0)))
    counts_pad = jnp.pad(observed_count, ((1, 1),))
    values_pad = jnp.pad(observed_value, ((1, 1), (0, 0)))
    variance_pad = jnp.pad(error_variance, ((1, 1), (0, 0)), constant_values=1.0)
    weights_matrix = region_transform(
        three_bands.astype(jnp.float32),
        lax.dynamic_slice_in_dim(cells_pad, parallel_strip, 3, 0),
        lax.dynamic_slice_in_dim(counts_pad, parallel_strip, 3, 0),
        lax.dynamic_slice_in_dim(values_pad, parallel_strip, 3, 0),
        lax.dynamic_slice_in_dim(variance_pad, parallel_strip, 3, 0),
        lax.dynamic_slice_in_dim(radius, parallel_strip, 1, 0)[0],
        parallel_strip - 1,
        patch_fourth,
        rows_here,
        lon_total,
        lon_total // mem_count,
        NS_ITERS,
    )
    folded = weights_matrix + (1.0 - jnp.sum(weights_matrix, axis=0, keepdims=True)) / members
    folded = folded.reshape(mem_count, CHUNKS, group, members).transpose(1, 0, 2, 3)
    folded = folded.reshape(members, members)
    coarse = folded.astype(bf)
    fine = (folded - coarse.astype(jnp.float32)).astype(bf)
    third = fields // 3
    updated = call(
        mix_kernel,
        (3,),
        [pl.BlockSpec((mem_count, third, pairs, group, 128), lambda i: (0, i, 0, 0, 0))] * CHUNKS
        + [whole((2 * members, members))],
        jax.ShapeDtypeStruct((fields, rows_here, lon_total // mem_count, members), bf),
        pl.BlockSpec((third, rows_here, lon_total // mem_count, members), lambda i: (i, 0, 0, 0)),
        (),
        4 * members * members * fields * 256,
        members * fields * 1024,
    )(*arrived, jnp.concatenate([coarse, fine], axis=0))
    return updated.transpose(3, 0, 1, 2)


def solution(mesh):
    return jax.shard_map(
        body,
        mesh=mesh,
        in_specs=(P("mem", None, "reg", None), P(), P(), P(), P(), P(), P(), P(), P(), P()),
        out_specs=P(None, None, "reg", "mem"),
        check_vma=False,
    )
```
